768 devices in a mesh: dp: 192 (over y, z, core), mp: 4 (over x).
Axes of the slice: x: 4, y: 8, z: 12, core: 2. Of those that a mesh axis runs over, the one named last changes fastest.
Arguments:
- activations: bfloat16 [192, 256, 2048], P('dp'), may hold values from -6 to 6
- output_grads: bfloat16 [192, 256, 2048], P('dp', None, 'mp'), may hold values from -8 to 8, as said below
- error_in: bfloat16 [192, 2048, 2048], P('dp', None, 'mp'), may hold values from -3 to 3
- start_basis: float32 [32, 2048], P(None, 'mp'), may hold values from -6 to 6
Outputs:
- new_error: bfloat16 [192, 2048, 2048], P('dp', None, 'mp')
- update: bfloat16 [2048, 2048], P(None, 'mp')
The draws below stay inside these ranges and needn't reach their ends.
Inputs may be any that keep to these rules, and one draw needn't show every extreme that they name: `output_grads`: real values.
All inputs are finite; a program needn't handle non-finite values.
Results may differ from the reference program's by a relative error of at most 0.002.
Values sent between devices are 32-bit elements; how exact they have to be, the bound alone decides.
A program may use at most 32 MiB of HBM per device.

```python
import math
import jax
import jax.numpy as jnp
from jax import lax

IN = 2048
OUT = 2048
RANK = 32
TOK = 256
REPLICAS = 192


def draw_output_grads(key, part):
    key = jax.random.fold_in(key, 7)
    key_base, key_rows, key_cols = jax.random.split(key, 3)
    base_draw = jax.random.truncated_normal(key_base, -4.0, 4.0, (REPLICAS, TOK, OUT), jnp.float32)
    row_scale = jnp.exp(jax.random.uniform(key_rows, (REPLICAS, TOK, 1), jnp.float32, 0.0, math.log(3.0)))
    column_scale = jnp.exp(jax.random.uniform(key_cols, (1, 1, OUT), jnp.float32, 0.0, math.log(3.0)))
    column_ramp = 1.0 + 1.2 * jnp.arange(OUT, dtype=jnp.float32) / OUT
    values = base_draw * row_scale * column_scale * column_ramp / (6.0 * math.sqrt(TOK))
    return values.astype(jnp.bfloat16)


def level_of(stream_key, extent, cuts, least, largest):
    gain = 1.0
    for position, blocks in cuts:
        heights = jax.random.uniform(jax.random.fold_in(jax.random.fold_in(stream_key, 6), position), (blocks,), jnp.float32, least / len(cuts), largest / len(cuts))
        gain = gain * jnp.repeat(jnp.exp(heights), extent[position] // blocks).reshape((-1,) + (1,) * (len(extent) - 1 - position))
    return gain


def noise(stream_key, extent, scale, most, cuts=(), kind=jnp.bfloat16):
    result = jax.random.normal(stream_key, extent, jnp.float32) * scale
    if len(cuts) > 0:
        result = level_of(stream_key, extent, cuts, -0.22, 0.18) * result
    return jnp.clip(result, min=-most, max=most).astype(kind)


def setup_inputs(seed: int = 0) -> dict:
    arg_keys = jax.random.split(jax.random.key(seed), 5)
    return {
        "activations": noise(arg_keys[0], (REPLICAS, TOK, IN), 1.0, 6.0, ((0, 192),)),
        "output_grads": draw_output_grads(jax.random.fold_in(arg_keys[4], 71), 0),
        "error_in": noise(arg_keys[2], (REPLICAS, IN, OUT), 0.5, 3.0, ((0, 192), (2, 4))),
        "start_basis": noise(arg_keys[3], (RANK, OUT), 1.0, 6.0, ((1, 4),), jnp.float32),
    }


clip_scale = 1.5

def orthonormalize(left_factor):
    gram_matrix = jnp.dot(left_factor.astype(jnp.float32), left_factor.T.astype(jnp.float32), precision=lax.Precision.HIGHEST, preferred_element_type=jnp.float32)
    lower_factor = jnp.linalg.cholesky(gram_matrix)
    return lax.linalg.triangular_solve(lower_factor, left_factor, left_side=True, lower=True)

def reference(activations, output_grads, error_in, start_basis):
    highest = lax.Precision.HIGHEST

    def left_step(running, scan_items):
        act_block, grad_block, error_block = scan_items
        through = jnp.dot(start_basis, grad_block.astype(jnp.float32).T, precision=highest)
        left_term = jnp.dot(through, act_block.astype(jnp.float32), precision=highest)
        left_term = left_term + jnp.dot(start_basis, error_block.astype(jnp.float32).T, precision=highest)
        return (running + left_term, None)
    left_factor, unused = lax.scan(left_step, jnp.zeros((RANK, IN), jnp.float32), (activations, output_grads, error_in))
    ortho_basis = orthonormalize(left_factor)

    def right_step(running, scan_items):
        act_block, grad_block, error_block = scan_items
        through = jnp.dot(ortho_basis, act_block.astype(jnp.float32).T, precision=highest)
        right_term = jnp.dot(through, grad_block.astype(jnp.float32), precision=highest)
        right_term = right_term + jnp.dot(ortho_basis, error_block.astype(jnp.float32), precision=highest)
        return (running + right_term, None)
    right_factor, unused = lax.scan(right_step, jnp.zeros((RANK, OUT), jnp.float32), (activations, output_grads, error_in))
    decompressed = jnp.dot(ortho_basis.T, right_factor, precision=highest)
    total_norm = jnp.sqrt(jnp.sum(right_factor * right_factor))
    limit = clip_scale * math.sqrt(REPLICAS * RANK * OUT)
    ratio = total_norm / limit
    clip_factor = 1.0 / jnp.sqrt(1.0 + ratio * ratio)

    def error_step(scan_items):
        act_block, grad_block, error_block = scan_items
        gradient = jnp.dot(act_block.T.astype(jnp.float32), grad_block.astype(jnp.float32), preferred_element_type=jnp.float32)
        return (gradient + error_block.astype(jnp.float32) - decompressed / REPLICAS).astype(jnp.bfloat16)
    new_error = lax.map(error_step, (activations, output_grads, error_in))
    update = (clip_factor * decompressed).astype(jnp.bfloat16)
    return (new_error, update)
```

```python
import functools
import math

import jax
import jax.numpy as jnp
from jax import lax
from jax.experimental import pallas as pl
from jax.experimental.pallas import tpu as pltpu
from jax.sharding import PartitionSpec as P

clip_scale = 1.5

GRID = (8, 12, 2)

MESH = pl.DeviceIdType.MESH
F32 = jnp.float32
BF16 = jnp.bfloat16
LANES = 128
NT = (((1,), (1,)), ((), ()))
NN = (((1,), (0,)), ((), ()))
TN = (((0,), (0,)), ((), ()))
PHASES = 11
A_CORE, A_SPLIT, A_LINE, A_JOIN, A_CORE2, B_CORE, B_SPLIT, B_LINE, B_JOIN, B_CORE2, NORM = range(PHASES)


def dot(a, b, dims):
    return lax.dot_general(a, b, dims, preferred_element_type=F32)


def exact_dot(a, b, dims):
    return lax.dot_general(a, b, dims, precision=lax.Precision.HIGHEST, preferred_element_type=F32)


def pieces(value):
    first = value.astype(BF16)
    rest = value - first.astype(F32)
    second = rest.astype(BF16)
    third = (rest - second.astype(F32)).astype(BF16)
    return first, second, third


def stack(value):
    return jnp.concatenate(pieces(value), axis=0)


def unstack(value):
    rows = value.shape[0] // 3
    return (value[2 * rows :] + value[rows : 2 * rows]) + value[:rows]


def ring_offsets(sizes):
    offsets = [()]
    for size in sizes:
        offsets = [o + (k,) for o in offsets for k in range(size)]
    far = lambda o: sum(min(k, s - k) for k, s in zip(o, sizes))
    return sorted([o for o in offsets if any(o)], key=lambda o: -far(o))


def kernel(
    xs, ys, zs, cs, limit,
    act_hbm, grad_hbm, err_hbm, basis_hbm,
    err_out, upd_out,
    act, grad, err, basis, acc,
    a_term, a_core, a_sum, a_split, a_line, left, left_t,
    b_term, b_core, b_split, b_line, right, norm,
    in_sem, send_sem, recv_sem,
):
    replica, x = lax.axis_index("dp"), lax.axis_index("mp")
    y, z, c = replica // (zs * cs), (replica // cs) % zs, replica % cs
    other = 1 - c
    half_in = act.shape[2]
    half_out = grad.shape[2]
    ranks = basis.shape[0]

    def at(px, py, pz, pc):
        return ((py * zs + pz) * cs + pc, px)

    def load(source, target, k):
        copy = pltpu.make_async_copy(source, target, in_sem.at[k])
        copy.start()
        return copy

    copies = {"basis": load(basis_hbm, basis, 0)}
    for q in range(cs):
        copies["grad", q] = load(grad_hbm.at[0, :, pl.ds(q * half_out, half_out)], grad.at[q], 1 + q)
    k = 1 + cs
    for place, h in enumerate((other, c)):
        cols = pl.ds(pl.multiple_of(h * half_in, LANES), half_in)
        copies["act", place] = load(act_hbm.at[0, :, cols], act.at[h], k)
        rows = pl.ds(pl.multiple_of(h * half_in, LANES), half_in)
        for q in range(cs):
            copies["err", place, q] = load(
                err_hbm.at[0, rows, pl.ds(q * half_out, half_out)], err.at[h, q], k + 1 + q
            )
        k += 1 + cs

    plane = [((x + ox) % xs, (y + oy) % ys) for ox, oy in ring_offsets((xs, ys))]
    column = [(y + oy) % ys for (oy,) in ring_offsets((ys,))]
    line = [(z + oz) % zs for (oz,) in ring_offsets((zs,))]
    row = [(x + ox) % xs for (ox,) in ring_offsets((xs,))]
    partners = [at(px, py, z, c) for px, py in plane] + [at(x, y, pz, c) for pz in line]
    partners += [at(x, y, z, other)]
    barrier = pltpu.get_barrier_semaphore()
    for partner in partners:
        pl.semaphore_signal(barrier, inc=1, device_id=partner, device_id_type=MESH)

    def send(source, target, phase, device):
        pltpu.make_async_remote_copy(
            src_ref=source,
            dst_ref=target,
            send_sem=send_sem.at[phase],
            recv_sem=recv_sem.at[phase],
            device_id=device,
            device_id_type=MESH,
        ).start()

    def arrived(phase, like):
        pltpu.make_async_copy(like, like, recv_sem.at[phase]).wait()

    def sent(phase, like):
        pltpu.make_async_copy(like, like, send_sem.at[phase]).wait()

    copies["basis"].wait()
    basis_parts = [stack(basis[:, q * half_out : (q + 1) * half_out]) for q in range(cs)]
    through = jnp.zeros((3 * ranks, grad.shape[1]), F32)
    for q in range(cs):
        copies["grad", q].wait()
        through += dot(basis_parts[q], grad[q], NT)
    through = stack(unstack(through))

    def left_term(place, h):
        copies["act", place].wait()
        term = dot(through, act[h], NN)
        for q in range(cs):
            copies["err", place, q].wait()
            term += dot(basis_parts[q], err[h, q], NT)
        term = unstack(term)
        width = a_term.shape[4]
        for py in range(ys):
            a_term[h, py] = term[:, py * width : (py + 1) * width].reshape(a_term.shape[2:])

    left_term(0, other)
    pl.semaphore_wait(barrier, len(partners))
    send(a_term.at[other], a_core, A_CORE, at(x, y, z, other))
    left_term(1, c)
    arrived(A_CORE, a_core)
    a_sum[...] = a_term[c] + a_core[...]

    me = y * xs + x
    for px, py in plane:
        send(a_sum.at[py, px], a_split.at[me], A_SPLIT, at(px, py, z, c))
    a_split[me] = a_sum[y, x]

    for h in range(cs):
        for q in range(cs):
            acc[h, q] = dot(act[h], grad[q], TN) + err[h, q].astype(F32)

    arrived(A_SPLIT, a_split.at[pl.ds(0, xs * ys - 1)])
    a_line[z] = jnp.sum(a_split[...], axis=0)
    for pz in line:
        send(a_line.at[z], a_line.at[z], A_LINE, at(x, y, pz, c))
    arrived(A_LINE, a_line.at[pl.ds(0, zs - 1)])
    left[c, y, x] = jnp.sum(a_line[...], axis=0)
    for px, py in plane:
        send(left.at[c, y, x], left.at[c, y, x], A_JOIN, at(px, py, z, c))
    arrived(A_JOIN, a_split.at[pl.ds(0, xs * ys - 1)])
    send(left.at[c], left.at[c], A_CORE2, at(x, y, z, other))
    arrived(A_CORE2, left.at[0])

    left_parts = []
    for h in range(cs):
        blocks = [left[h, py].reshape(ranks, left.shape[4]) for py in range(ys)]
        left_parts.append(pieces(jnp.concatenate(blocks, axis=1)))
    left_stacks = [jnp.concatenate(p, axis=0) for p in left_parts]
    through = jnp.zeros((3 * ranks, grad.shape[1]), F32)
    for h in range(cs):
        through += dot(left_stacks[h], act[h], NT)
    through = stack(unstack(through))

    b_rows = b_term.shape[2]
    b_wide = half_out // LANES

    def right_term(q):
        term = dot(through, grad[q], NN)
        for h in range(cs):
            term += dot(left_stacks[h], err[h, q], NN)
        term = unstack(term)
        for p in range(ys):
            i, j = p // b_wide, p % b_wide
            b_term[q, p] = term[i * b_rows : (i + 1) * b_rows, j * LANES : (j + 1) * LANES]

    right_term(other)
    send(b_term.at[other], b_core, B_CORE, at(x, y, z, other))
    right_term(c)
    arrived(B_CORE, b_core)
    b_core[...] = b_term[c] + b_core[...]
    for py in column:
        send(b_core.at[py], b_split.at[y], B_SPLIT, at(x, py, z, c))
    b_split[y] = b_core[y]

    gram = jnp.zeros((ranks, ranks), F32)
    for first, second, third in left_parts:
        low = dot(jnp.concatenate([first, second], axis=0), second, NT)
        gram += dot(first, third, NT) + dot(third, first, NT)
        gram += low[:ranks] + low[ranks:]
        gram += dot(second, first, NT)
    for first, second, third in left_parts:
        gram += dot(first, first, NT)
    at_row = lax.broadcasted_iota(jnp.int32, (ranks, ranks), 0)
    at_col = lax.broadcasted_iota(jnp.int32, (ranks, ranks), 1)
    inverse = (at_row == at_col).astype(F32)
    for j in range(ranks - 1):
        factor = gram[:, j : j + 1] / gram[j : j + 1, j : j + 1]
        factor = jnp.where(at_row > j, factor, 0.0)
        gram = gram - factor * gram[j : j + 1, :]
        inverse = inverse - factor * inverse[j : j + 1, :]
    pivots = jnp.sum(jnp.where(at_row == at_col, gram, 0.0), axis=1, keepdims=True)
    inverse = inverse / jnp.sqrt(pivots)

    arrived(B_SPLIT, b_split.at[pl.ds(0, ys - 1)])
    b_line[z] = jnp.sum(b_split[...], axis=0)
    for pz in line:
        send(b_line.at[z], b_line.at[z], B_LINE, at(x, y, pz, c))

    for h in range(cs):
        one, two, three = left_parts[h]
        blank = jnp.zeros((2 * ranks, half_in), BF16)
        rows6 = jnp.concatenate([one, one, one, two, two, three, blank], axis=0)
        left_t[h] = rows6.T

    arrived(B_LINE, b_line.at[pl.ds(0, zs - 1)])
    right[c, y] = jnp.sum(b_line[...], axis=0)
    for py in column:
        send(right.at[c, y], right.at[c, y], B_JOIN, at(x, py, z, c))
    arrived(B_JOIN, right.at[0, pl.ds(0, ys - 1)])
    send(right.at[c], right.at[c], B_CORE2, at(x, y, z, other))
    arrived(B_CORE2, right.at[0])

    halves = []
    for q in range(cs):
        lines = [
            jnp.concatenate([right[q, i * b_wide + j] for j in range(b_wide)], axis=1)
            for i in range(ys // b_wide)
        ]
        halves.append(jnp.concatenate(lines, axis=0))
    raw = jnp.concatenate(halves, axis=1)
    factor = exact_dot(inverse, raw, NN)
    squares = jnp.sum((factor * factor).reshape(ranks // 8, 8, cs * half_out), axis=0)
    squares = sum(squares[:, j * LANES : (j + 1) * LANES] for j in range(cs * b_wide))
    norm[x] = squares
    for px in row:
        send(norm.at[x], norm.at[x], NORM, at(px, y, z, c))

    weights = exact_dot(inverse, factor, TN)
    one, two, three = pieces(weights)
    blank = jnp.zeros((2 * ranks, cs * half_out), BF16)
    weights = jnp.concatenate([one, two, three, one, two, one, blank], axis=0)
    replicas = ys * zs * cs
    for h in range(cs):
        for q in range(cs):
            cols = slice(q * half_out, (q + 1) * half_out)
            whole = dot(left_t[h], weights[:, cols], NN)
            err_out[h * half_in : (h + 1) * half_in, cols] = (acc[h, q] - whole / replicas).astype(BF16)
            acc[h, q] = whole

    arrived(NORM, norm.at[pl.ds(0, xs - 1)])
    total = jnp.sum(norm[...], axis=0)
    total = jnp.sum(jnp.sum(total, axis=0, keepdims=True), axis=1, keepdims=True)
    ratio = jnp.sqrt(total) / limit
    clip = 1.0 / jnp.sqrt(1.0 + ratio * ratio)
    for h in range(cs):
        for q in range(cs):
            cols = slice(q * half_out, (q + 1) * half_out)
            upd_out[h * half_in : (h + 1) * half_in, cols] = (clip * acc[h, q]).astype(BF16)

    sent(A_CORE, a_core)
    sent(A_SPLIT, a_split.at[pl.ds(0, xs * ys - 1)])
    sent(A_LINE, a_line.at[pl.ds(0, zs - 1)])
    sent(A_JOIN, a_split.at[pl.ds(0, xs * ys - 1)])
    sent(A_CORE2, left.at[0])
    sent(B_CORE, b_core)
    sent(B_SPLIT, b_split.at[pl.ds(0, ys - 1)])
    sent(B_LINE, b_line.at[pl.ds(0, zs - 1)])
    sent(B_JOIN, right.at[0, pl.ds(0, ys - 1)])
    sent(B_CORE2, right.at[0])
    sent(NORM, norm.at[pl.ds(0, xs - 1)])


def per_device(activations, output_grads, error_in, start_basis):
    ys, zs, cs = GRID
    xs = lax.axis_size("mp")
    tokens, features = activations.shape[1:]
    width = output_grads.shape[2]
    ranks = start_basis.shape[0]
    half_in, half_out = features // cs, width // cs
    limit = clip_scale * math.sqrt(ys * zs * cs * ranks * width * xs)
    a_piece = (ranks // xs, half_in // ys)
    b_piece = (ranks * half_out // ys // LANES, LANES)
    outs = pl.pallas_call(
        functools.partial(kernel, xs, ys, zs, cs, limit),
        out_shape=[pltpu.VMEM((features, width), BF16)] * 2,
        in_specs=[pl.BlockSpec(memory_space=pl.ANY)] * 4,
        out_specs=[pl.BlockSpec(memory_space=pltpu.VMEM)] * 2,
        scratch_shapes=[
            pltpu.VMEM((cs, tokens, half_in), BF16),
            pltpu.VMEM((cs, tokens, half_out), BF16),
            pltpu.VMEM((cs, cs, half_in, half_out), BF16),
            pltpu.VMEM((ranks, width), F32),
            pltpu.VMEM((cs, cs, half_in, half_out), F32),
            pltpu.VMEM((cs, ys, xs) + a_piece, F32),
            pltpu.VMEM((ys, xs) + a_piece, F32),
            pltpu.VMEM((ys, xs) + a_piece, F32),
            pltpu.VMEM((ys * xs,) + a_piece, F32),
            pltpu.VMEM((zs,) + a_piece, F32),
            pltpu.VMEM((cs, ys, xs) + a_piece, F32),
            pltpu.VMEM((cs, half_in, 8 * ranks), BF16),
            pltpu.VMEM((cs, ys) + b_piece, F32),
            pltpu.VMEM((ys,) + b_piece, F32),
            pltpu.VMEM((ys,) + b_piece, F32),
            pltpu.VMEM((zs,) + b_piece, F32),
            pltpu.VMEM((cs, ys) + b_piece, F32),
            pltpu.VMEM((xs, 8, LANES), F32),
            pltpu.SemaphoreType.DMA((1 + cs + cs * (1 + cs),)),
            pltpu.SemaphoreType.DMA((PHASES,)),
            pltpu.SemaphoreType.DMA((PHASES,)),
        ],
        compiler_params=pltpu.CompilerParams(
            collective_id=0, has_side_effects=True, vmem_limit_bytes=58 * 2**20
        ),
        name="compress",
    )(activations, output_grads, error_in, start_basis)
    return outs[0][None], outs[1]


def solution(mesh):
    in_specs = (P("dp", None, None), P("dp", None, "mp"), P("dp", None, "mp"), P(None, "mp"))
    out_specs = (P("dp", None, "mp"), P(None, "mp"))
    return jax.shard_map(
        per_device, mesh=mesh, in_specs=in_specs, out_specs=out_specs, check_vma=False
    )
```

```python
import functools
import math

import jax
import jax.numpy as jnp
from jax import lax
from jax.experimental import pallas as pl
from jax.experimental.pallas import tpu as pltpu
from jax.sharding import PartitionSpec as P

clip_scale = 1.5

GRID = (8, 12, 2)

MESH = pl.DeviceIdType.MESH
F32 = jnp.float32
BF16 = jnp.bfloat16
LANES = 128
ROWS = 8
NT = (((1,), (1,)), ((), ()))
NN = (((1,), (0,)), ((), ()))
TN = (((0,), (0,)), ((), ()))
PHASES = 10
A_CORE, A_SPLIT, A_LINE, A_JOIN, A_TWIN, B_SPLIT, B_LINE, B_CORE, B_JOIN, NORM = range(PHASES)


def dot(a, b, dims):
    return lax.dot_general(a, b, dims, preferred_element_type=F32)


def exact_dot(a, b, dims):
    return lax.dot_general(a, b, dims, precision=lax.Precision.HIGHEST, preferred_element_type=F32)


def pieces(value):
    first = value.astype(BF16)
    rest = value - first.astype(F32)
    second = rest.astype(BF16)
    third = (rest - second.astype(F32)).astype(BF16)
    return first, second, third


def stack(value):
    return jnp.concatenate(pieces(value), axis=0)


def unstack(value):
    rows = value.shape[0] // 3
    return (value[2 * rows :] + value[rows : 2 * rows]) + value[:rows]


def pack(value):
    return jnp.concatenate([value[r : r + ROWS] for r in range(0, value.shape[0], ROWS)], axis=1)


def unpack(value, columns):
    return jnp.concatenate([value[:, j : j + columns] for j in range(0, value.shape[1], columns)], axis=0)


def ring(offset, size):
    return min(offset, size - offset)


def ring_offsets(sizes):
    offsets = [()]
    for size in sizes:
        offsets = [o + (k,) for o in offsets for k in range(size)]
    far = lambda o: sum(ring(k, s) for k, s in zip(o, sizes))
    return sorted([o for o in offsets if any(o)], key=lambda o: -far(o))


def reduce_kernel(
    xs, ys, zs, cs, limit,
    act_hbm, grad_hbm, err_hbm, basis_hbm,
    err_out, whole_out, clip_out,
    act, grad, err, basis, acc,
    a_term, a_core, a_split, a_line, left, left_t,
    b_term, b_split, b_line, b_mine, b_core, right, norm,
    in_sem, send_sem, recv_sem,
):
    replica, x = lax.axis_index("dp"), lax.axis_index("mp")
    y, z, c = replica // (zs * cs), (replica // cs) % zs, replica % cs
    ranks, width = basis.shape
    depth = act.shape[2]
    half = depth // cs
    far = ys // 2

    def at(px, py, pz, pc):
        return ((py * zs + pz) * cs + pc, px)

    plane = [((x + ox) % xs, (y + oy) % ys, ring(oy, ys)) for ox, oy in ring_offsets((xs, ys))]
    column = [(y + oy) % ys for (oy,) in ring_offsets((ys,))]
    line = [(z + oz) % zs for (oz,) in ring_offsets((zs,))]
    twin = at(x, y, z, 1 - c)
    partners = [at(x, y, pz, c) for pz in line[:3]] + [at(px, py, z, c) for px, py, _ in plane]
    partners += [at(x, y, pz, c) for pz in line[3:]] + [twin]
    barrier = pltpu.get_barrier_semaphore()
    for partner in partners:
        pl.semaphore_signal(barrier, inc=1, device_id=partner, device_id_type=MESH)

    loads = []

    def load(source, target):
        copy = pltpu.make_async_copy(source, target, in_sem.at[len(loads)])
        copy.start()
        loads.append(copy)

    load(basis_hbm, basis)
    load(grad_hbm.at[0], grad)
    for py in range(ys):
        load(act_hbm.at[0, :, pl.ds(py * depth, depth)], act.at[py])
    for py in range(ys):
        load(err_hbm.at[py], err.at[py])

    def send(source, target, phase, device, arrival=None):
        pltpu.make_async_remote_copy(
            src_ref=source,
            dst_ref=target,
            send_sem=send_sem.at[phase],
            recv_sem=recv_sem.at[phase if arrival is None else arrival],
            device_id=device,
            device_id_type=MESH,
        ).start()

    def arrived(phase, like):
        pltpu.make_async_copy(like, like, recv_sem.at[phase]).wait()

    def sent(phase, like):
        pltpu.make_async_copy(like, like, send_sem.at[phase]).wait()

    loads[0].wait()
    loads[1].wait()
    basis_parts = stack(basis[...])
    through = stack(unstack(dot(basis_parts, grad[...], NT)))
    for py in range(ys):
        loads[2 + py].wait()
        loads[2 + ys + py].wait()
        term = unstack(dot(through, act[py], NN) + dot(basis_parts, err[py], NT))
        for h in range(cs):
            a_term[h, py] = term[:, h * half : (h + 1) * half].reshape(a_term.shape[2:])

    pl.semaphore_wait(barrier, len(partners))
    me = y * xs + x
    send(a_term.at[1 - c], a_core, A_CORE, twin)
    arrived(A_CORE, a_core)
    a_core[...] = a_term[c] + a_core[...]
    for px, py, _ in plane:
        send(a_core.at[py, px], a_split.at[me], A_SPLIT, at(px, py, z, c))
    a_split[me] = a_core[y, x]

    for py in range(ys):
        acc[py] = dot(act[py], grad[...], TN) + err[py].astype(F32)

    others = xs * ys - 1
    arrived(A_SPLIT, a_split.at[pl.ds(0, others)])
    a_line[z] = jnp.sum(a_split[...], axis=0)
    for pz in line:
        send(a_line.at[z], a_line.at[z], A_LINE, at(x, y, pz, c))
    arrived(A_LINE, a_line.at[pl.ds(0, zs - 1)])
    left[c, y, x] = jnp.sum(a_line[...], axis=0)
    for px, py, distance in plane:
        send(left.at[c, y, x], left.at[c, y, x], A_JOIN, at(px, py, z, c), PHASES + distance)

    def left_block(py):
        return jnp.concatenate([left[h, py].reshape(ranks, half) for h in range(cs)], axis=1)

    through = jnp.zeros((3 * ranks, grad.shape[0]), F32)
    term = jnp.zeros((3 * ranks, width), F32)
    for distance in range(far + 2):
        if distance <= far:
            rows = [oy for oy in range(ys) if ring(oy, ys) == distance]
            count = len(rows) * xs - (distance == 0)
            arrived(PHASES + distance, a_split.at[pl.ds(0, count)])
            for oy in rows:
                mine = left.at[c, (y + oy) % ys]
                send(mine, mine, A_TWIN, twin, PHASES + far + 1 + distance)
        if distance > 0:
            rows = [oy for oy in range(ys) if ring(oy, ys) == distance - 1]
            arrived(PHASES + far + distance, a_split.at[pl.ds(0, len(rows) * xs)])
            for oy in rows:
                py = (y + oy) % ys
                block = stack(left_block(py))
                through += dot(block, act[py], NT)
                term += dot(block, err[py], NN)
    term = unstack(term + dot(stack(unstack(through)), grad[...], NN))
    columns = width // ys
    for py in range(ys):
        b_term[py] = pack(term[:, py * columns : (py + 1) * columns])

    for py in column:
        send(b_term.at[py], b_split.at[y], B_SPLIT, at(x, py, z, c))
    b_split[y] = b_term[y]

    gram = jnp.zeros((ranks, ranks), F32)
    for py in range(ys):
        first, second, third = pieces(left_block(py))
        low = dot(jnp.concatenate([first, second], axis=0), second, NT)
        gram += (dot(first, third, NT) + dot(third, first, NT)) + (low[ranks:] + low[:ranks])
        gram += dot(second, first, NT)
        gram += dot(first, first, NT)
    at_row = lax.broadcasted_iota(jnp.int32, (ranks, ranks), 0)
    at_col = lax.broadcasted_iota(jnp.int32, (ranks, ranks), 1)
    inverse = (at_row == at_col).astype(F32)
    for j in range(ranks - 1):
        factor = gram[:, j : j + 1] / gram[j : j + 1, j : j + 1]
        factor = jnp.where(at_row > j, factor, 0.0)
        gram = gram - factor * gram[j : j + 1, :]
        inverse = inverse - factor * inverse[j : j + 1, :]
    pivots = jnp.sum(jnp.where(at_row == at_col, gram, 0.0), axis=1, keepdims=True)
    inverse = inverse / jnp.sqrt(pivots)

    arrived(B_SPLIT, b_split.at[pl.ds(0, ys - 1)])
    b_line[z] = jnp.sum(b_split[...], axis=0)
    for pz in line:
        send(b_line.at[z], b_line.at[z], B_LINE, at(x, y, pz, c))

    for py in range(ys):
        one, two, three = pieces(left_block(py))
        blank = jnp.zeros((2 * ranks, depth), BF16)
        left_t[py] = jnp.concatenate([one, one, one, two, two, three, blank], axis=0).T

    arrived(B_LINE, b_line.at[pl.ds(0, zs - 1)])
    b_mine[...] = jnp.sum(b_line[...], axis=0)
    send(b_mine, b_core, B_CORE, twin)
    arrived(B_CORE, b_core)
    right[y] = b_mine[...] + b_core[...]
    for py in column:
        send(right.at[y], right.at[y], B_JOIN, at(x, py, z, c))

    factor = exact_dot(inverse, unpack(right[y], columns), NN)
    squares = jnp.sum((factor * factor).reshape(ranks // ROWS, ROWS, columns), axis=0)
    if columns < LANES:
        squares = jnp.concatenate([squares, jnp.zeros((ROWS, LANES - columns), F32)], axis=1)
    else:
        squares = sum(squares[:, j : j + LANES] for j in range(0, columns, LANES))
    norm[me] = squares
    for px, py, _ in plane:
        send(norm.at[me], norm.at[me], NORM, at(px, py, z, c))

    arrived(B_JOIN, right.at[pl.ds(0, ys - 1)])
    raw = jnp.concatenate([unpack(right[py], columns) for py in range(ys)], axis=1)
    weights = exact_dot(inverse, exact_dot(inverse, raw, NN), TN)
    one, two, three = pieces(weights)
    blank = jnp.zeros((2 * ranks, width), BF16)
    weights = jnp.concatenate([one, two, three, one, two, one, blank], axis=0)
    replicas = ys * zs * cs
    for py in range(ys):
        whole = dot(left_t[py], weights, NN)
        err_out[py] = (acc[py] - whole / replicas).astype(BF16)
        whole_out[py] = whole

    arrived(NORM, norm.at[pl.ds(0, others)])
    total = jnp.sum(norm[...], axis=0)
    total = jnp.sum(jnp.sum(total, axis=0, keepdims=True), axis=1, keepdims=True)
    ratio = jnp.sqrt(total) / limit
    clip_out[...] = jnp.broadcast_to(1.0 / jnp.sqrt(1.0 + ratio * ratio), clip_out.shape)

    sent(A_CORE, a_core)
    sent(A_SPLIT, a_split.at[pl.ds(0, others)])
    sent(A_LINE, a_line.at[pl.ds(0, zs - 1)])
    sent(A_JOIN, a_split.at[pl.ds(0, others)])
    sent(A_TWIN, left.at[0])
    sent(B_SPLIT, b_split.at[pl.ds(0, ys - 1)])
    sent(B_LINE, b_line.at[pl.ds(0, zs - 1)])
    sent(B_CORE, b_core)
    sent(B_JOIN, right.at[pl.ds(0, ys - 1)])
    sent(NORM, norm.at[pl.ds(0, others)])


def write_kernel(err_in, whole, clip, err_hbm, upd_hbm, upd, sem):
    blocks, depth, width = whole.shape
    copies = []

    def store(source, target):
        copies.append(pltpu.make_async_copy(source, target, sem.at[len(copies)]))
        copies[-1].start()

    for k in range(blocks):
        store(err_in.at[k], err_hbm.at[0, pl.ds(k * depth, depth)])
    scale = clip[:1, :1]
    for k in range(blocks):
        upd[k] = (scale * whole[k]).astype(BF16)
        store(upd.at[k], upd_hbm.at[pl.ds(k * depth, depth)])
    for copy in copies:
        copy.wait()


def per_device(activations, output_grads, error_in, start_basis):
    ys, zs, cs = GRID
    xs = lax.axis_size("mp")
    tokens, features = activations.shape[1:]
    width = output_grads.shape[2]
    ranks = start_basis.shape[0]
    depth = features // ys
    limit = clip_scale * math.sqrt(ys * zs * cs * ranks * width * xs)
    a_piece = (ranks // xs, depth // cs)
    b_piece = (ROWS, ranks // ROWS * (width // ys))
    in_vmem = pl.BlockSpec(memory_space=pltpu.VMEM)
    in_hbm = pl.BlockSpec(memory_space=pl.ANY)
    new_error, whole, clip = pl.pallas_call(
        functools.partial(reduce_kernel, xs, ys, zs, cs, limit),
        out_shape=[
            pltpu.VMEM((ys, depth, width), BF16),
            pltpu.VMEM((ys, depth, width), F32),
            pltpu.VMEM((ROWS, LANES), F32),
        ],
        in_specs=[in_hbm] * 4,
        out_specs=[in_vmem] * 3,
        scratch_shapes=[
            pltpu.VMEM((ys, tokens, depth), BF16),
            pltpu.VMEM((tokens, width), BF16),
            pltpu.VMEM((ys, depth, width), BF16),
            pltpu.VMEM((ranks, width), F32),
            pltpu.VMEM((ys, depth, width), F32),
            pltpu.VMEM((cs, ys, xs) + a_piece, F32),
            pltpu.VMEM((ys, xs) + a_piece, F32),
            pltpu.VMEM((ys * xs,) + a_piece, F32),
            pltpu.VMEM((zs,) + a_piece, F32),
            pltpu.VMEM((cs, ys, xs) + a_piece, F32),
            pltpu.VMEM((ys, depth, 8 * ranks), BF16),
            pltpu.VMEM((ys,) + b_piece, F32),
            pltpu.VMEM((ys,) + b_piece, F32),
            pltpu.VMEM((zs,) + b_piece, F32),
            pltpu.VMEM(b_piece, F32),
            pltpu.VMEM(b_piece, F32),
            pltpu.VMEM((ys,) + b_piece, F32),
            pltpu.VMEM((ys * xs, ROWS, LANES), F32),
            pltpu.SemaphoreType.DMA((2 + 2 * ys,)),
            pltpu.SemaphoreType.DMA((PHASES,)),
            pltpu.SemaphoreType.DMA((PHASES + 2 * (ys // 2 + 1),)),
        ],
        compiler_params=pltpu.CompilerParams(
            collective_id=0, has_side_effects=True, vmem_limit_bytes=56 * 2**20
        ),
        name="reduce",
    )(activations, output_grads, error_in.reshape(ys, depth, width), start_basis)
    return pl.pallas_call(
        write_kernel,
        out_shape=[
            jax.ShapeDtypeStruct((1, features, width), BF16),
            jax.ShapeDtypeStruct((features, width), BF16),
        ],
        in_specs=[in_vmem] * 3,
        out_specs=[in_hbm] * 2,
        scratch_shapes=[
            pltpu.VMEM((ys, depth, width), BF16),
            pltpu.SemaphoreType.DMA((2 * ys,)),
        ],
        compiler_params=pltpu.CompilerParams(vmem_limit_bytes=16 * 2**20),
        name="write",
    )(new_error, whole, clip)


def solution(mesh):
    in_specs = (P("dp", None, None), P("dp", None, "mp"), P("dp", None, "mp"), P(None, "mp"))
    out_specs = (P("dp", None, "mp"), P(None, "mp"))
    return jax.shard_map(
        per_device, mesh=mesh, in_specs=in_specs, out_specs=out_specs, check_vma=False
    )
```

```python
import functools
import math

import jax
import jax.numpy as jnp
from jax import lax
from jax.experimental import pallas as pl
from jax.experimental.pallas import tpu as pltpu
from jax.sharding import PartitionSpec as P

clip_scale = 1.5

GRID = (8, 12, 2)

MESH = pl.DeviceIdType.MESH
F32 = jnp.float32
BF16 = jnp.bfloat16
LANES = 128
ROWS = 8
NT = (((1,), (1,)), ((), ()))
NN = (((1,), (0,)), ((), ()))
TN = (((0,), (0,)), ((), ()))
PHASES = 10
A_CORE, A_SPLIT, A_LINE, A_JOIN, A_TWIN, B_SPLIT, B_LINE, B_CORE, B_JOIN, NORM = range(PHASES)


def dot(a, b, dims):
    return lax.dot_general(a, b, dims, preferred_element_type=F32)


def exact_dot(a, b, dims):
    return lax.dot_general(a, b, dims, precision=lax.Precision.HIGHEST, preferred_element_type=F32)


def pieces(value):
    first = value.astype(BF16)
    rest = value - first.astype(F32)
    second = rest.astype(BF16)
    third = (rest - second.astype(F32)).astype(BF16)
    return first, second, third


def stack(value):
    return jnp.concatenate(pieces(value), axis=0)


def unstack(value):
    rows = value.shape[0] // 3
    return (value[2 * rows :] + value[rows : 2 * rows]) + value[:rows]


def pack(value):
    return jnp.concatenate([value[r : r + ROWS] for r in range(0, value.shape[0], ROWS)], axis=1)


def unpack(value, columns):
    return jnp.concatenate([value[:, j : j + columns] for j in range(0, value.shape[1], columns)], axis=0)


def ring(offset, size):
    return min(offset, size - offset)


def ring_offsets(sizes):
    offsets = [()]
    for size in sizes:
        offsets = [o + (k,) for o in offsets for k in range(size)]
    far = lambda o: sum(ring(k, s) for k, s in zip(o, sizes))
    return sorted([o for o in offsets if any(o)], key=lambda o: -far(o))


def reduce_kernel(
    xs, ys, zs, cs, limit,
    act_hbm, grad_hbm, err_hbm, basis_hbm,
    err_out, whole_out, clip_out,
    act, grad, err, basis, acc,
    a_term, a_core, a_split, a_line, left, left_t,
    b_term, b_split, b_line, b_mine, b_core, right, norm,
    in_sem, send_sem, recv_sem,
):
    replica, x = lax.axis_index("dp"), lax.axis_index("mp")
    y, rest = lax.div(replica, zs * cs), lax.rem(replica, zs * cs)
    z, c = lax.div(rest, cs), lax.rem(rest, cs)
    ranks, width = basis.shape
    depth = act.shape[2]
    half = depth // cs
    far = ys // 2

    def at(px, py, pz, pc):
        return ((py * zs + pz) * cs + pc, px)

    along_x = [lax.rem(x + ox, xs) for ox in range(xs)]
    along_y = [lax.rem(y + oy, ys) for oy in range(ys)]
    along_z = [lax.rem(z + oz, zs) for oz in range(zs)]
    plane = [(along_x[ox], along_y[oy], ring(oy, ys)) for ox, oy in ring_offsets((xs, ys))]
    column = [along_y[oy] for (oy,) in ring_offsets((ys,))]
    line = [along_z[oz] for (oz,) in ring_offsets((zs,))]
    twin = at(x, y, z, 1 - c)
    partners = [at(x, y, pz, c) for pz in line[:3]] + [at(px, py, z, c) for px, py, _ in plane]
    partners += [at(x, y, pz, c) for pz in line[3:]] + [twin]
    barrier = pltpu.get_barrier_semaphore()
    for partner in partners:
        pl.semaphore_signal(barrier, inc=1, device_id=partner, device_id_type=MESH)

    def load(source, target, k):
        pltpu.make_async_copy(source, target, in_sem.at[k]).start()

    def loaded(target, k):
        pltpu.make_async_copy(target, target, in_sem.at[k]).wait()

    load(basis_hbm, basis, 0)
    load(grad_hbm.at[0], grad, 1)
    for py in range(ys):
        load(act_hbm.at[0, :, pl.ds(py * depth, depth)], act.at[py], 2)
    load(err_hbm, err, 3)

    def send(source, target, phase, device, arrival=None):
        pltpu.make_async_remote_copy(
            src_ref=source,
            dst_ref=target,
            send_sem=send_sem.at[phase],
            recv_sem=recv_sem.at[phase if arrival is None else arrival],
            device_id=device,
            device_id_type=MESH,
        ).start()

    def arrived(phase, like):
        pltpu.make_async_copy(like, like, recv_sem.at[phase]).wait()

    def sent(phase, like):
        pltpu.make_async_copy(like, like, send_sem.at[phase]).wait()

    loaded(basis, 0)
    loaded(grad, 1)
    basis_parts = stack(basis[...])
    through = stack(unstack(dot(basis_parts, grad[...], NT)))
    loaded(act, 2)
    loaded(err, 3)
    for py in range(ys):
        term = unstack(dot(through, act[py], NN) + dot(basis_parts, err[py], NT))
        for h in range(cs):
            a_term[h, py] = term[:, h * half : (h + 1) * half].reshape(a_term.shape[2:])

    pl.semaphore_wait(barrier, len(partners))
    me = y * xs + x
    send(a_term.at[1 - c], a_core, A_CORE, twin)
    arrived(A_CORE, a_core)
    a_core[...] = a_term[c] + a_core[...]
    for px, py, _ in plane:
        send(a_core.at[py, px], a_split.at[me], A_SPLIT, at(px, py, z, c))
    a_split[me] = a_core[y, x]

    for py in range(ys):
        acc[py] = dot(act[py], grad[...], TN) + err[py].astype(F32)

    others = xs * ys - 1
    arrived(A_SPLIT, a_split.at[pl.ds(0, others)])
    a_line[z] = jnp.sum(a_split[...], axis=0)
    for pz in line:
        send(a_line.at[z], a_line.at[z], A_LINE, at(x, y, pz, c))
    arrived(A_LINE, a_line.at[pl.ds(0, zs - 1)])
    left[c, y, x] = jnp.sum(a_line[...], axis=0)
    for px, py, distance in plane:
        send(left.at[c, y, x], left.at[c, y, x], A_JOIN, at(px, py, z, c), PHASES + distance)

    def left_block(py):
        return jnp.concatenate([left[h, py].reshape(ranks, half) for h in range(cs)], axis=1)

    through = jnp.zeros((3 * ranks, grad.shape[0]), F32)
    term = jnp.zeros((3 * ranks, width), F32)
    for distance in range(far + 3):
        if distance <= far:
            rows = [oy for oy in range(ys) if ring(oy, ys) == distance]
            count = len(rows) * xs - (distance == 0)
            arrived(PHASES + distance, a_split.at[pl.ds(0, count)])
            for oy in rows:
                mine = left.at[c, along_y[oy]]
                send(mine, mine, A_TWIN, twin, PHASES + far + 1 + distance)
        if distance > 1:
            rows = [oy for oy in range(ys) if ring(oy, ys) == distance - 2]
            arrived(PHASES + far + distance - 1, a_split.at[pl.ds(0, len(rows) * xs)])
            for oy in rows:
                py = along_y[oy]
                block = stack(left_block(py))
                through += dot(block, act[py], NT)
                term += dot(block, err[py], NN)
    term = unstack(term + dot(stack(unstack(through)), grad[...], NN))
    columns = width // ys
    for py in range(ys):
        b_term[py] = pack(term[:, py * columns : (py + 1) * columns])

    for py in column:
        send(b_term.at[py], b_split.at[y], B_SPLIT, at(x, py, z, c))
    b_split[y] = b_term[y]

    gram = jnp.zeros((ranks, ranks), F32)
    for py in range(ys):
        first, second, third = pieces(left_block(py))
        low = dot(jnp.concatenate([first, second], axis=0), second, NT)
        gram += (dot(first, third, NT) + dot(third, first, NT)) + (low[ranks:] + low[:ranks])
        gram += dot(second, first, NT)
        gram += dot(first, first, NT)
    at_row = lax.broadcasted_iota(jnp.int32, (ranks, ranks), 0)
    at_col = lax.broadcasted_iota(jnp.int32, (ranks, ranks), 1)
    inverse = (at_row == at_col).astype(F32)
    for j in range(ranks - 1):
        factor = gram[:, j : j + 1] / gram[j : j + 1, j : j + 1]
        factor = jnp.where(at_row > j, factor, 0.0)
        gram = gram - factor * gram[j : j + 1, :]
        inverse = inverse - factor * inverse[j : j + 1, :]
    pivots = jnp.sum(jnp.where(at_row == at_col, gram, 0.0), axis=1, keepdims=True)
    inverse = inverse / jnp.sqrt(pivots)

    arrived(B_SPLIT, b_split.at[pl.ds(0, ys - 1)])
    b_line[z] = jnp.sum(b_split[...], axis=0)
    for pz in line:
        send(b_line.at[z], b_line.at[z], B_LINE, at(x, y, pz, c))

    for py in range(ys):
        one, two, three = pieces(left_block(py))
        blank = jnp.zeros((2 * ranks, depth), BF16)
        left_t[py] = jnp.concatenate([one, one, one, two, two, three, blank], axis=0).T

    arrived(B_LINE, b_line.at[pl.ds(0, zs - 1)])
    b_mine[...] = jnp.sum(b_line[...], axis=0)
    send(b_mine, b_core, B_CORE, twin)
    arrived(B_CORE, b_core)
    right[y] = b_mine[...] + b_core[...]
    for py in column:
        send(right.at[y], right.at[y], B_JOIN, at(x, py, z, c))

    factor = exact_dot(inverse, unpack(right[y], columns), NN)
    squares = jnp.sum((factor * factor).reshape(ranks // ROWS, ROWS, columns), axis=0)
    if columns < LANES:
        squares = jnp.concatenate([squares, jnp.zeros((ROWS, LANES - columns), F32)], axis=1)
    else:
        squares = sum(squares[:, j : j + LANES] for j in range(0, columns, LANES))
    norm[me] = squares
    for px, py, _ in plane:
        send(norm.at[me], norm.at[me], NORM, at(px, py, z, c))

    arrived(B_JOIN, right.at[pl.ds(0, ys - 1)])
    raw = jnp.concatenate([unpack(right[py], columns) for py in range(ys)], axis=1)
    weights = exact_dot(inverse, exact_dot(inverse, raw, NN), TN)
    one, two, three = pieces(weights)
    blank = jnp.zeros((2 * ranks, width), BF16)
    weights = jnp.concatenate([one, two, three, one, two, one, blank], axis=0)
    replicas = ys * zs * cs
    for py in range(ys):
        whole = dot(left_t[py], weights, NN)
        err_out[py] = (acc[py] - whole / replicas).astype(BF16)
        whole_out[py] = whole

    arrived(NORM, norm.at[pl.ds(0, others)])
    total = jnp.sum(norm[...], axis=0)
    total = jnp.sum(jnp.sum(total, axis=0, keepdims=True), axis=1, keepdims=True)
    ratio = jnp.sqrt(total) / limit
    clip_out[...] = jnp.broadcast_to(1.0 / jnp.sqrt(1.0 + ratio * ratio), clip_out.shape)

    sent(A_CORE, a_core)
    sent(A_SPLIT, a_split.at[pl.ds(0, others)])
    sent(A_LINE, a_line.at[pl.ds(0, zs - 1)])
    sent(A_JOIN, a_split.at[pl.ds(0, others)])
    sent(A_TWIN, left.at[0])
    sent(B_SPLIT, b_split.at[pl.ds(0, ys - 1)])
    sent(B_LINE, b_line.at[pl.ds(0, zs - 1)])
    sent(B_CORE, b_core)
    sent(B_JOIN, right.at[pl.ds(0, ys - 1)])
    sent(NORM, norm.at[pl.ds(0, others)])


def write_kernel(err_in, whole, clip, err_hbm, upd_hbm, upd, sem):
    blocks, depth, width = whole.shape
    copies = []

    def store(source, target):
        copies.append(pltpu.make_async_copy(source, target, sem.at[len(copies)]))
        copies[-1].start()

    for k in range(blocks):
        store(err_in.at[k], err_hbm.at[0, pl.ds(k * depth, depth)])
    scale = clip[:1, :1]
    for k in range(blocks):
        upd[k] = (scale * whole[k]).astype(BF16)
        store(upd.at[k], upd_hbm.at[pl.ds(k * depth, depth)])
    for copy in copies:
        copy.wait()


def per_device(activations, output_grads, error_in, start_basis):
    ys, zs, cs = GRID
    xs = lax.axis_size("mp")
    tokens, features = activations.shape[1:]
    width = output_grads.shape[2]
    ranks = start_basis.shape[0]
    depth = features // ys
    limit = clip_scale * math.sqrt(ys * zs * cs * ranks * width * xs)
    a_piece = (ranks // xs, depth // cs)
    b_piece = (ROWS, ranks // ROWS * (width // ys))
    in_vmem = pl.BlockSpec(memory_space=pltpu.VMEM)
    in_hbm = pl.BlockSpec(memory_space=pl.ANY)
    new_error, whole, clip = pl.pallas_call(
        functools.partial(reduce_kernel, xs, ys, zs, cs, limit),
        out_shape=[
            pltpu.VMEM((ys, depth, width), BF16),
            pltpu.VMEM((ys, depth, width), F32),
            pltpu.VMEM((ROWS, LANES), F32),
        ],
        in_specs=[in_hbm] * 4,
        out_specs=[in_vmem] * 3,
        scratch_shapes=[
            pltpu.VMEM((ys, tokens, depth), BF16),
            pltpu.VMEM((tokens, width), BF16),
            pltpu.VMEM((ys, depth, width), BF16),
            pltpu.VMEM((ranks, width), F32),
            pltpu.VMEM((ys, depth, width), F32),
            pltpu.VMEM((cs, ys, xs) + a_piece, F32),
            pltpu.VMEM((ys, xs) + a_piece, F32),
            pltpu.VMEM((ys * xs,) + a_piece, F32),
            pltpu.VMEM((zs,) + a_piece, F32),
            pltpu.VMEM((cs, ys, xs) + a_piece, F32),
            pltpu.VMEM((ys, depth, 8 * ranks), BF16),
            pltpu.VMEM((ys,) + b_piece, F32),
            pltpu.VMEM((ys,) + b_piece, F32),
            pltpu.VMEM((zs,) + b_piece, F32),
            pltpu.VMEM(b_piece, F32),
            pltpu.VMEM(b_piece, F32),
            pltpu.VMEM((ys,) + b_piece, F32),
            pltpu.VMEM((ys * xs, ROWS, LANES), F32),
            pltpu.SemaphoreType.DMA((4,)),
            pltpu.SemaphoreType.DMA((PHASES,)),
            pltpu.SemaphoreType.DMA((PHASES + 2 * (ys // 2 + 1),)),
        ],
        compiler_params=pltpu.CompilerParams(
            collective_id=0, has_side_effects=True, vmem_limit_bytes=56 * 2**20
        ),
        name="reduce",
    )(activations, output_grads, error_in.reshape(ys, depth, width), start_basis)
    return pl.pallas_call(
        write_kernel,
        out_shape=[
            jax.ShapeDtypeStruct((1, features, width), BF16),
            jax.ShapeDtypeStruct((features, width), BF16),
        ],
        in_specs=[in_vmem] * 3,
        out_specs=[in_hbm] * 2,
        scratch_shapes=[
            pltpu.VMEM((ys, depth, width), BF16),
            pltpu.SemaphoreType.DMA((2 * ys,)),
        ],
        compiler_params=pltpu.CompilerParams(vmem_limit_bytes=16 * 2**20),
        name="write",
    )(new_error, whole, clip)


def solution(mesh):
    in_specs = (P("dp", None, None), P("dp", None, "mp"), P("dp", None, "mp"), P(None, "mp"))
    out_specs = (P("dp", None, "mp"), P(None, "mp"))
    return jax.shard_map(
        per_device, mesh=mesh, in_specs=in_specs, out_specs=out_specs, check_vma=False
    )
```

```python
import functools
import math

import jax
import jax.numpy as jnp
from jax import lax
from jax.experimental import pallas as pl
from jax.experimental.pallas import tpu as pltpu
from jax.sharding import PartitionSpec as P

clip_scale = 1.5

GRID = (8, 12, 2)

MESH = pl.DeviceIdType.MESH
F32 = jnp.float32
BF16 = jnp.bfloat16
LANES = 128
ROWS = 8
NT = (((1,), (1,)), ((), ()))
NN = (((1,), (0,)), ((), ()))
TN = (((0,), (0,)), ((), ()))
PHASES = 10
A_CORE, A_SPLIT, A_LINE, A_JOIN, A_TWIN, B_SPLIT, B_LINE, B_CORE, B_JOIN, NORM = range(PHASES)


def dot(a, b, dims):
    return lax.dot_general(a, b, dims, preferred_element_type=F32)


def exact_dot(a, b, dims):
    return lax.dot_general(a, b, dims, precision=lax.Precision.HIGHEST, preferred_element_type=F32)


def pieces(value):
    first = value.astype(BF16)
    rest = value - first.astype(F32)
    second = rest.astype(BF16)
    third = (rest - second.astype(F32)).astype(BF16)
    return first, second, third


def stack(value):
    return jnp.concatenate(pieces(value), axis=0)


def unstack(value):
    rows = value.shape[0] // 3
    return (value[2 * rows :] + value[rows : 2 * rows]) + value[:rows]


def pack(value):
    return jnp.concatenate([value[r : r + ROWS] for r in range(0, value.shape[0], ROWS)], axis=1)


def unpack(value, columns):
    return jnp.concatenate([value[:, j : j + columns] for j in range(0, value.shape[1], columns)], axis=0)


def ring(offset, size):
    return min(offset, size - offset)


def ring_offsets(sizes):
    offsets = [()]
    for size in sizes:
        offsets = [o + (k,) for o in offsets for k in range(size)]
    far = lambda o: sum(ring(k, s) for k, s in zip(o, sizes))
    return sorted([o for o in offsets if any(o)], key=lambda o: -far(o))


def reduce_kernel(
    xs, ys, zs, cs,
    act_hbm, grad_hbm, err_hbm, basis_hbm,
    err_out, whole_out, total_out,
    act, grad, err, basis, acc,
    a_term, a_core, a_split, a_line, left, left_t,
    b_term, b_split, b_line, b_mine, b_core, right, norm,
    in_sem, send_sem, recv_sem,
):
    replica, x = lax.axis_index("dp"), lax.axis_index("mp")
    y, rest = lax.div(replica, zs * cs), lax.rem(replica, zs * cs)
    z, c = lax.div(rest, cs), lax.rem(rest, cs)
    ranks, width = basis.shape
    depth = act.shape[2]
    half = depth // cs
    far = ys // 2

    def at(px, py, pz, pc):
        return ((py * zs + pz) * cs + pc, px)

    along_x = [lax.rem(x + ox, xs) for ox in range(xs)]
    along_y = [lax.rem(y + oy, ys) for oy in range(ys)]
    along_z = [lax.rem(z + oz, zs) for oz in range(zs)]
    plane = [(along_x[ox], along_y[oy], ring(oy, ys)) for ox, oy in ring_offsets((xs, ys))]
    column = [along_y[oy] for (oy,) in ring_offsets((ys,))]
    line = [along_z[oz] for (oz,) in ring_offsets((zs,))]
    twin = at(x, y, z, 1 - c)
    partners = [at(x, y, pz, c) for pz in line[:3]] + [at(px, py, z, c) for px, py, _ in plane]
    partners += [at(x, y, pz, c) for pz in line[3:]] + [twin]
    barrier = pltpu.get_barrier_semaphore()
    for partner in partners:
        pl.semaphore_signal(barrier, inc=1, device_id=partner, device_id_type=MESH)

    def load(source, target, k):
        pltpu.make_async_copy(source, target, in_sem.at[k]).start()

    def loaded(target, k):
        pltpu.make_async_copy(target, target, in_sem.at[k]).wait()

    load(basis_hbm, basis, 0)
    load(grad_hbm.at[0], grad, 1)
    for py in range(ys):
        load(act_hbm.at[0, :, pl.ds(py * depth, depth)], act.at[py], 2)
    load(err_hbm, err, 3)

    def send(source, target, phase, device, arrival=None):
        pltpu.make_async_remote_copy(
            src_ref=source,
            dst_ref=target,
            send_sem=send_sem.at[phase],
            recv_sem=recv_sem.at[phase if arrival is None else arrival],
            device_id=device,
            device_id_type=MESH,
        ).start()

    def arrived(phase, like):
        pltpu.make_async_copy(like, like, recv_sem.at[phase]).wait()

    def sent(phase, like):
        pltpu.make_async_copy(like, like, send_sem.at[phase]).wait()

    loaded(basis, 0)
    loaded(grad, 1)
    basis_parts = stack(basis[...])
    through = stack(unstack(dot(basis_parts, grad[...], NT)))
    loaded(act, 2)
    loaded(err, 3)
    for py in range(ys):
        term = unstack(dot(through, act[py], NN) + dot(basis_parts, err[py], NT))
        for h in range(cs):
            a_term[h, py] = term[:, h * half : (h + 1) * half].reshape(a_term.shape[2:])

    pl.semaphore_wait(barrier, len(partners))
    me = y * xs + x
    send(a_term.at[1 - c], a_core, A_CORE, twin)
    arrived(A_CORE, a_core)
    a_core[...] = a_term[c] + a_core[...]
    for px, py, _ in plane:
        send(a_core.at[py, px], a_split.at[me], A_SPLIT, at(px, py, z, c))
    a_split[me] = a_core[y, x]

    for py in range(ys):
        acc[py] = dot(act[py], grad[...], TN) + err[py].astype(F32)

    others = xs * ys - 1
    arrived(A_SPLIT, a_split.at[pl.ds(0, others)])
    a_line[z] = jnp.sum(a_split[...], axis=0)
    for pz in line:
        send(a_line.at[z], a_line.at[z], A_LINE, at(x, y, pz, c))
    arrived(A_LINE, a_line.at[pl.ds(0, zs - 1)])
    left[c, y, x] = jnp.sum(a_line[...], axis=0)
    for px, py, distance in plane:
        send(left.at[c, y, x], left.at[c, y, x], A_JOIN, at(px, py, z, c), PHASES + distance)

    def left_block(py):
        return jnp.concatenate([left[h, py].reshape(ranks, half) for h in range(cs)], axis=1)

    through = jnp.zeros((3 * ranks, grad.shape[0]), F32)
    term = jnp.zeros((3 * ranks, width), F32)
    for distance in range(far + 3):
        if distance <= far:
            rows = [oy for oy in range(ys) if ring(oy, ys) == distance]
            count = len(rows) * xs - (distance == 0)
            arrived(PHASES + distance, a_split.at[pl.ds(0, count)])
            for oy in rows:
                mine = left.at[c, along_y[oy]]
                send(mine, mine, A_TWIN, twin, PHASES + far + 1 + distance)
        if distance > 1:
            rows = [oy for oy in range(ys) if ring(oy, ys) == distance - 2]
            arrived(PHASES + far + distance - 1, a_split.at[pl.ds(0, len(rows) * xs)])
            for oy in rows:
                py = along_y[oy]
                block = stack(left_block(py))
                through += dot(block, act[py], NT)
                term += dot(block, err[py], NN)
    term = unstack(term + dot(stack(unstack(through)), grad[...], NN))
    columns = width // ys
    for py in range(ys):
        b_term[py] = pack(term[:, py * columns : (py + 1) * columns])

    for py in column:
        send(b_term.at[py], b_split.at[y], B_SPLIT, at(x, py, z, c))
    b_split[y] = b_term[y]

    gram = jnp.zeros((ranks, ranks), F32)
    for py in range(ys):
        first, second, third = pieces(left_block(py))
        low = dot(jnp.concatenate([first, second], axis=0), second, NT)
        gram += (dot(first, third, NT) + dot(third, first, NT)) + (low[ranks:] + low[:ranks])
        gram += dot(second, first, NT)
        gram += dot(first, first, NT)
    at_row = lax.broadcasted_iota(jnp.int32, (ranks, ranks), 0)
    at_col = lax.broadcasted_iota(jnp.int32, (ranks, ranks), 1)
    inverse = (at_row == at_col).astype(F32)
    for j in range(ranks - 1):
        factor = gram[:, j : j + 1] / gram[j : j + 1, j : j + 1]
        factor = jnp.where(at_row > j, factor, 0.0)
        gram = gram - factor * gram[j : j + 1, :]
        inverse = inverse - factor * inverse[j : j + 1, :]
    pivots = jnp.sum(jnp.where(at_row == at_col, gram, 0.0), axis=1, keepdims=True)
    inverse = inverse / jnp.sqrt(pivots)

    arrived(B_SPLIT, b_split.at[pl.ds(0, ys - 1)])
    b_line[z] = jnp.sum(b_split[...], axis=0)
    for pz in line:
        send(b_line.at[z], b_line.at[z], B_LINE, at(x, y, pz, c))

    for py in range(ys):
        one, two, three = pieces(left_block(py))
        blank = jnp.zeros((2 * ranks, depth), BF16)
        left_t[py] = jnp.concatenate([one, one, one, two, two, three, blank], axis=0).T

    arrived(B_LINE, b_line.at[pl.ds(0, zs - 1)])
    b_mine[...] = jnp.sum(b_line[...], axis=0)
    send(b_mine, b_core, B_CORE, twin)
    arrived(B_CORE, b_core)
    right[y] = b_mine[...] + b_core[...]
    for py in column:
        send(right.at[y], right.at[y], B_JOIN, at(x, py, z, c))

    factor = exact_dot(inverse, unpack(right[y], columns), NN)
    squares = jnp.sum(factor * factor, axis=0, keepdims=True)
    if columns < LANES:
        squares = jnp.concatenate([squares, jnp.zeros((1, LANES - columns), F32)], axis=1)
    else:
        squares = sum(squares[:, j : j + LANES] for j in range(0, columns, LANES))
    norm[me] = squares
    for px, py, _ in plane:
        send(norm.at[me], norm.at[me], NORM, at(px, py, z, c))

    arrived(B_JOIN, right.at[pl.ds(0, ys - 1)])
    raw = jnp.concatenate([unpack(right[py], columns) for py in range(ys)], axis=1)
    weights = exact_dot(inverse, exact_dot(inverse, raw, NN), TN)
    one, two, three = pieces(weights)
    blank = jnp.zeros((2 * ranks, width), BF16)
    weights = jnp.concatenate([one, two, three, one, two, one, blank], axis=0)
    replicas = ys * zs * cs
    for py in range(ys):
        whole = dot(left_t[py], weights, NN)
        err_out[py] = (acc[py] - whole / replicas).astype(BF16)
        whole_out[py] = whole

    sent(A_CORE, a_core)
    sent(A_SPLIT, a_split.at[pl.ds(0, others)])
    sent(A_LINE, a_line.at[pl.ds(0, zs - 1)])
    sent(A_JOIN, a_split.at[pl.ds(0, others)])
    sent(A_TWIN, left.at[0])
    sent(B_SPLIT, b_split.at[pl.ds(0, ys - 1)])
    sent(B_LINE, b_line.at[pl.ds(0, zs - 1)])
    sent(B_CORE, b_core)
    sent(B_JOIN, right.at[pl.ds(0, ys - 1)])
    sent(NORM, norm.at[pl.ds(0, others)])
    arrived(NORM, norm.at[pl.ds(0, others)])
    total_out[...] = jnp.sum(norm[...], axis=0)


def write_kernel(limit, err_in, whole, total, err_hbm, upd_hbm, upd, sem):
    blocks, depth, width = whole.shape
    copies = []

    def store(source, target):
        copies.append(pltpu.make_async_copy(source, target, sem.at[len(copies)]))
        copies[-1].start()

    for k in range(blocks):
        store(err_in.at[k], err_hbm.at[0, pl.ds(k * depth, depth)])
    ratio = jnp.sqrt(jnp.sum(total[...], axis=1, keepdims=True)) / limit
    clip = 1.0 / jnp.sqrt(1.0 + ratio * ratio)
    for k in range(blocks):
        upd[k] = (clip * whole[k]).astype(BF16)
        store(upd.at[k], upd_hbm.at[pl.ds(k * depth, depth)])
    for copy in copies:
        copy.wait()


def per_device(activations, output_grads, error_in, start_basis):
    ys, zs, cs = GRID
    xs = lax.axis_size("mp")
    tokens, features = activations.shape[1:]
    width = output_grads.shape[2]
    ranks = start_basis.shape[0]
    depth = features // ys
    limit = clip_scale * math.sqrt(ys * zs * cs * ranks * width * xs)
    a_piece = (ranks // xs, depth // cs)
    b_piece = (ROWS, ranks // ROWS * (width // ys))
    in_vmem = pl.BlockSpec(memory_space=pltpu.VMEM)
    in_hbm = pl.BlockSpec(memory_space=pl.ANY)
    new_error, whole, total = pl.pallas_call(
        functools.partial(reduce_kernel, xs, ys, zs, cs),
        out_shape=[
            pltpu.VMEM((ys, depth, width), BF16),
            pltpu.VMEM((ys, depth, width), F32),
            pltpu.VMEM((1, LANES), F32),
        ],
        in_specs=[in_hbm] * 4,
        out_specs=[in_vmem] * 3,
        scratch_shapes=[
            pltpu.VMEM((ys, tokens, depth), BF16),
            pltpu.VMEM((tokens, width), BF16),
            pltpu.VMEM((ys, depth, width), BF16),
            pltpu.VMEM((ranks, width), F32),
            pltpu.VMEM((ys, depth, width), F32),
            pltpu.VMEM((cs, ys, xs) + a_piece, F32),
            pltpu.VMEM((ys, xs) + a_piece, F32),
            pltpu.VMEM((ys * xs,) + a_piece, F32),
            pltpu.VMEM((zs,) + a_piece, F32),
            pltpu.VMEM((cs, ys, xs) + a_piece, F32),
            pltpu.VMEM((ys, depth, 8 * ranks), BF16),
            pltpu.VMEM((ys,) + b_piece, F32),
            pltpu.VMEM((ys,) + b_piece, F32),
            pltpu.VMEM((zs,) + b_piece, F32),
            pltpu.VMEM(b_piece, F32),
            pltpu.VMEM(b_piece, F32),
            pltpu.VMEM((ys,) + b_piece, F32),
            pltpu.VMEM((ys * xs, 1, LANES), F32),
            pltpu.SemaphoreType.DMA((4,)),
            pltpu.SemaphoreType.DMA((PHASES,)),
            pltpu.SemaphoreType.DMA((PHASES + 2 * (ys // 2 + 1),)),
        ],
        compiler_params=pltpu.CompilerParams(
            collective_id=0, has_side_effects=True, vmem_limit_bytes=56 * 2**20
        ),
        name="reduce",
    )(activations, output_grads, error_in.reshape(ys, depth, width), start_basis)
    return pl.pallas_call(
        functools.partial(write_kernel, limit),
        out_shape=[
            jax.ShapeDtypeStruct((1, features, width), BF16),
            jax.ShapeDtypeStruct((features, width), BF16),
        ],
        in_specs=[in_vmem] * 3,
        out_specs=[in_hbm] * 2,
        scratch_shapes=[
            pltpu.VMEM((ys, depth, width), BF16),
            pltpu.SemaphoreType.DMA((2 * ys,)),
        ],
        compiler_params=pltpu.CompilerParams(vmem_limit_bytes=16 * 2**20),
        name="write",
    )(new_error, whole, total)


def solution(mesh):
    in_specs = (P("dp", None, None), P("dp", None, "mp"), P("dp", None, "mp"), P(None, "mp"))
    out_specs = (P("dp", None, "mp"), P(None, "mp"))
    return jax.shard_map(
        per_device, mesh=mesh, in_specs=in_specs, out_specs=out_specs, check_vma=False
    )
```

```python
import functools
import math

import jax
import jax.numpy as jnp
from jax import lax
from jax.experimental import pallas as pl
from jax.experimental.pallas import tpu as pltpu
from jax.sharding import PartitionSpec as P

clip_scale = 1.5

GRID = (8, 12, 2)

MESH = pl.DeviceIdType.MESH
F32 = jnp.float32
BF16 = jnp.bfloat16
LANES = 128
ROWS = 8
NT = (((1,), (1,)), ((), ()))
NN = (((1,), (0,)), ((), ()))
TN = (((0,), (0,)), ((), ()))
PHASES = 10
A_CORE, A_SPLIT, A_LINE, A_JOIN, A_TWIN, B_SPLIT, B_LINE, B_CORE, B_JOIN, NORM = range(PHASES)


def dot(a, b, dims):
    return lax.dot_general(a, b, dims, preferred_element_type=F32)


def exact_dot(a, b, dims):
    return lax.dot_general(a, b, dims, precision=lax.Precision.HIGHEST, preferred_element_type=F32)


def pieces(value):
    first = value.astype(BF16)
    rest = value - first.astype(F32)
    second = rest.astype(BF16)
    third = (rest - second.astype(F32)).astype(BF16)
    return first, second, third


def stack(value):
    return jnp.concatenate(pieces(value), axis=0)


def unstack(value):
    rows = value.shape[0] // 3
    return (value[2 * rows :] + value[rows : 2 * rows]) + value[:rows]


def pack(value):
    return jnp.concatenate([value[r : r + ROWS] for r in range(0, value.shape[0], ROWS)], axis=1)


def unpack(value, columns):
    return jnp.concatenate([value[:, j : j + columns] for j in range(0, value.shape[1], columns)], axis=0)


def ring(offset, size):
    return min(offset, size - offset)


def ring_offsets(sizes):
    offsets = [()]
    for size in sizes:
        offsets = [o + (k,) for o in offsets for k in range(size)]
    far = lambda o: sum(ring(k, s) for k, s in zip(o, sizes))
    return sorted([o for o in offsets if any(o)], key=lambda o: -far(o))


def reduce_kernel(
    xs, ys, zs, cs,
    act_hbm, grad_hbm, err_hbm, basis_hbm,
    err_out, whole_out, total_out,
    act, grad, err, basis, acc,
    a_term, a_core, a_split, a_line, left, left_t,
    b_term, b_split, b_line, b_mine, b_core, right, norm,
    in_sem, send_sem, recv_sem,
):
    replica, x = lax.axis_index("dp"), lax.axis_index("mp")
    y, rest = lax.div(replica, zs * cs), lax.rem(replica, zs * cs)
    z, c = lax.div(rest, cs), lax.rem(rest, cs)
    ranks, width = basis.shape
    depth = act.shape[2]
    half = depth // cs
    far = ys // 2

    def at(px, py, pz, pc):
        return ((py * zs + pz) * cs + pc, px)

    along_x = [lax.rem(x + ox, xs) for ox in range(xs)]
    along_y = [lax.rem(y + oy, ys) for oy in range(ys)]
    along_z = [lax.rem(z + oz, zs) for oz in range(zs)]
    plane = [(along_x[ox], along_y[oy], ring(oy, ys)) for ox, oy in ring_offsets((xs, ys))]
    column = [along_y[oy] for (oy,) in ring_offsets((ys,))]
    line = [along_z[oz] for (oz,) in ring_offsets((zs,))]
    twin = at(x, y, z, 1 - c)
    partners = [at(x, y, pz, c) for pz in line[:3]] + [at(px, py, z, c) for px, py, _ in plane]
    partners += [at(x, y, pz, c) for pz in line[3:]] + [twin]
    barrier = pltpu.get_barrier_semaphore()
    for partner in partners:
        pl.semaphore_signal(barrier, inc=1, device_id=partner, device_id_type=MESH)

    def load(source, target, k):
        pltpu.make_async_copy(source, target, in_sem.at[k]).start()

    def loaded(target, k):
        pltpu.make_async_copy(target, target, in_sem.at[k]).wait()

    load(basis_hbm, basis, 0)
    load(grad_hbm.at[0], grad, 1)
    for py in range(ys):
        load(act_hbm.at[0, :, pl.ds(py * depth, depth)], act.at[py], 2)
    load(err_hbm, err, 3)

    def send(source, target, phase, device, arrival=None):
        pltpu.make_async_remote_copy(
            src_ref=source,
            dst_ref=target,
            send_sem=send_sem.at[phase],
            recv_sem=recv_sem.at[phase if arrival is None else arrival],
            device_id=device,
            device_id_type=MESH,
        ).start()

    def arrived(phase, like):
        pltpu.make_async_copy(like, like, recv_sem.at[phase]).wait()

    def sent(phase, like):
        pltpu.make_async_copy(like, like, send_sem.at[phase]).wait()

    loaded(basis, 0)
    loaded(grad, 1)
    basis_parts = stack(basis[...])
    through = stack(unstack(dot(basis_parts, grad[...], NT)))
    loaded(act, 2)
    loaded(err, 3)
    for py in range(ys):
        term = unstack(dot(through, act[py], NN) + dot(basis_parts, err[py], NT))
        for h in range(cs):
            a_term[h, py] = term[:, h * half : (h + 1) * half].reshape(a_term.shape[2:])

    pl.semaphore_wait(barrier, len(partners))
    me = y * xs + x
    send(a_term.at[1 - c], a_core, A_CORE, twin)
    arrived(A_CORE, a_core)
    a_core[...] = a_term[c] + a_core[...]
    for px, py, _ in plane:
        send(a_core.at[py, px], a_split.at[me], A_SPLIT, at(px, py, z, c))
    a_split[me] = a_core[y, x]

    for py in range(ys):
        acc[py] = dot(act[py], grad[...], TN) + err[py].astype(F32)

    others = xs * ys - 1
    arrived(A_SPLIT, a_split.at[pl.ds(0, others)])
    a_line[z] = jnp.sum(a_split[...], axis=0)
    for pz in line:
        send(a_line.at[z], a_line.at[z], A_LINE, at(x, y, pz, c))
    arrived(A_LINE, a_line.at[pl.ds(0, zs - 1)])
    left[c, y, x] = jnp.sum(a_line[...], axis=0)
    for px, py, distance in plane:
        send(left.at[c, y, x], left.at[c, y, x], A_JOIN, at(px, py, z, c), PHASES + distance)

    def left_block(py):
        return jnp.concatenate([left[h, py].reshape(ranks, half) for h in range(cs)], axis=1)

    through = jnp.zeros((3 * ranks, grad.shape[0]), F32)
    term = jnp.zeros((3 * ranks, width), F32)
    for distance in range(far + 3):
        if distance <= far:
            rows = [oy for oy in range(ys) if ring(oy, ys) == distance]
            count = len(rows) * xs - (distance == 0)
            arrived(PHASES + distance, a_split.at[pl.ds(0, count)])
            for oy in rows:
                mine = left.at[c, along_y[oy]]
                send(mine, mine, A_TWIN, twin, PHASES + far + 1 + distance)
        if distance > 1:
            rows = [oy for oy in range(ys) if ring(oy, ys) == distance - 2]
            arrived(PHASES + far + distance - 1, a_split.at[pl.ds(0, len(rows) * xs)])
            for oy in rows:
                py = along_y[oy]
                block = stack(left_block(py))
                through += dot(block, act[py], NT)
                term += dot(block, err[py], NN)
    term = unstack(term + dot(stack(unstack(through)), grad[...], NN))
    columns = width // ys
    for py in range(ys):
        b_term[py] = pack(term[:, py * columns : (py + 1) * columns])

    for py in column:
        send(b_term.at[py], b_split.at[y], B_SPLIT, at(x, py, z, c))
    b_split[y] = b_term[y]

    gram = jnp.zeros((ranks, ranks), F32)
    for py in range(ys):
        first, second, third = pieces(left_block(py))
        low = dot(jnp.concatenate([first, second], axis=0), second, NT)
        gram += (dot(first, third, NT) + dot(third, first, NT)) + (low[ranks:] + low[:ranks])
        gram += dot(second, first, NT)
        gram += dot(first, first, NT)
    at_row = lax.broadcasted_iota(jnp.int32, (ranks, ranks), 0)
    at_col = lax.broadcasted_iota(jnp.int32, (ranks, ranks), 1)
    inverse = (at_row == at_col).astype(F32)
    for j in range(ranks - 1):
        factor = gram[:, j : j + 1] / gram[j : j + 1, j : j + 1]
        factor = jnp.where(at_row > j, factor, 0.0)
        gram = gram - factor * gram[j : j + 1, :]
        inverse = inverse - factor * inverse[j : j + 1, :]
    pivots = jnp.sum(jnp.where(at_row == at_col, gram, 0.0), axis=1, keepdims=True)
    inverse = inverse / jnp.sqrt(pivots)

    arrived(B_SPLIT, b_split.at[pl.ds(0, ys - 1)])
    b_line[z] = jnp.sum(b_split[...], axis=0)
    for pz in line:
        send(b_line.at[z], b_line.at[z], B_LINE, at(x, y, pz, c))

    for py in range(ys):
        one, two, three = pieces(left_block(py))
        blank = jnp.zeros((2 * ranks, depth), BF16)
        left_t[py] = jnp.concatenate([one, one, one, two, two, three, blank], axis=0).T

    arrived(B_LINE, b_line.at[pl.ds(0, zs - 1)])
    b_mine[...] = jnp.sum(b_line[...], axis=0)
    send(b_mine, b_core, B_CORE, twin)
    arrived(B_CORE, b_core)
    right[y] = b_mine[...] + b_core[...]
    for py in column:
        send(right.at[y], right.at[y], B_JOIN, at(x, py, z, c))

    factor = exact_dot(inverse, unpack(right[y], columns), NN)
    squares = jnp.sum(factor * factor, axis=0, keepdims=True)
    if columns < LANES:
        squares = jnp.concatenate([squares, jnp.zeros((1, LANES - columns), F32)], axis=1)
    else:
        squares = sum(squares[:, j : j + LANES] for j in range(0, columns, LANES))
    norm[me] = squares
    for px, py, _ in plane:
        send(norm.at[me], norm.at[me], NORM, at(px, py, z, c))

    arrived(B_JOIN, right.at[pl.ds(0, ys - 1)])
    raw = jnp.concatenate([unpack(right[py], columns) for py in range(ys)], axis=1)
    weights = exact_dot(inverse, exact_dot(inverse, raw, NN), TN)
    one, two, three = pieces(weights)
    blank = jnp.zeros((2 * ranks, width), BF16)
    weights = jnp.concatenate([one, two, three, one, two, one, blank], axis=0)
    replicas = ys * zs * cs
    for py in range(ys):
        whole = dot(left_t[py], weights, NN)
        err_out[py] = (acc[py] - whole / replicas).astype(BF16)
        whole_out[py] = whole

    sent(A_CORE, a_core)
    sent(A_SPLIT, a_split.at[pl.ds(0, others)])
    sent(A_LINE, a_line.at[pl.ds(0, zs - 1)])
    sent(A_JOIN, a_split.at[pl.ds(0, others)])
    sent(A_TWIN, left.at[0])
    sent(B_SPLIT, b_split.at[pl.ds(0, ys - 1)])
    sent(B_LINE, b_line.at[pl.ds(0, zs - 1)])
    sent(B_CORE, b_core)
    sent(B_JOIN, right.at[pl.ds(0, ys - 1)])
    sent(NORM, norm.at[pl.ds(0, others)])
    arrived(NORM, norm.at[pl.ds(0, others)])
    total_out[...] = jnp.sum(norm[...], axis=0)


def write_kernel(limit, err_in, whole, total, err_hbm, upd_hbm, upd, sem):
    blocks, depth, width = whole.shape

    def rows(k):
        return pl.ds(k * depth, depth)

    for k in range(blocks):
        pltpu.make_async_copy(err_in.at[k], err_hbm.at[0, rows(k)], sem.at[0]).start()
    ratio = jnp.sqrt(jnp.sum(total[...], axis=1, keepdims=True)) / limit
    clip = 1.0 / jnp.sqrt(1.0 + ratio * ratio)
    for k in range(blocks):
        upd[k] = (clip * whole[k]).astype(BF16)
        pltpu.make_async_copy(upd.at[k], upd_hbm.at[rows(k)], sem.at[1]).start()
    pltpu.make_async_copy(err_in, err_in, sem.at[0]).wait()
    pltpu.make_async_copy(upd, upd, sem.at[1]).wait()


def per_device(activations, output_grads, error_in, start_basis):
    ys, zs, cs = GRID
    xs = lax.axis_size("mp")
    tokens, features = activations.shape[1:]
    width = output_grads.shape[2]
    ranks = start_basis.shape[0]
    depth = features // ys
    limit = clip_scale * math.sqrt(ys * zs * cs * ranks * width * xs)
    a_piece = (ranks // xs, depth // cs)
    b_piece = (ROWS, ranks // ROWS * (width // ys))
    in_vmem = pl.BlockSpec(memory_space=pltpu.VMEM)
    in_hbm = pl.BlockSpec(memory_space=pl.ANY)
    new_error, whole, total = pl.pallas_call(
        functools.partial(reduce_kernel, xs, ys, zs, cs),
        out_shape=[
            pltpu.VMEM((ys, depth, width), BF16),
            pltpu.VMEM((ys, depth, width), F32),
            pltpu.VMEM((1, LANES), F32),
        ],
        in_specs=[in_hbm] * 4,
        out_specs=[in_vmem] * 3,
        scratch_shapes=[
            pltpu.VMEM((ys, tokens, depth), BF16),
            pltpu.VMEM((tokens, width), BF16),
            pltpu.VMEM((ys, depth, width), BF16),
            pltpu.VMEM((ranks, width), F32),
            pltpu.VMEM((ys, depth, width), F32),
            pltpu.VMEM((cs, ys, xs) + a_piece, F32),
            pltpu.VMEM((ys, xs) + a_piece, F32),
            pltpu.VMEM((ys * xs,) + a_piece, F32),
            pltpu.VMEM((zs,) + a_piece, F32),
            pltpu.VMEM((cs, ys, xs) + a_piece, F32),
            pltpu.VMEM((ys, depth, 8 * ranks), BF16),
            pltpu.VMEM((ys,) + b_piece, F32),
            pltpu.VMEM((ys,) + b_piece, F32),
            pltpu.VMEM((zs,) + b_piece, F32),
            pltpu.VMEM(b_piece, F32),
            pltpu.VMEM(b_piece, F32),
            pltpu.VMEM((ys,) + b_piece, F32),
            pltpu.VMEM((ys * xs, 1, LANES), F32),
            pltpu.SemaphoreType.DMA((4,)),
            pltpu.SemaphoreType.DMA((PHASES,)),
            pltpu.SemaphoreType.DMA((PHASES + 2 * (ys // 2 + 1),)),
        ],
        compiler_params=pltpu.CompilerParams(
            collective_id=0, has_side_effects=True, vmem_limit_bytes=56 * 2**20
        ),
        name="reduce",
    )(activations, output_grads, error_in.reshape(ys, depth, width), start_basis)
    return pl.pallas_call(
        functools.partial(write_kernel, limit),
        out_shape=[
            jax.ShapeDtypeStruct((1, features, width), BF16),
            jax.ShapeDtypeStruct((features, width), BF16),
        ],
        in_specs=[in_vmem] * 3,
        out_specs=[in_hbm] * 2,
        scratch_shapes=[
            pltpu.VMEM((ys, depth, width), BF16),
            pltpu.SemaphoreType.DMA((2,)),
        ],
        compiler_params=pltpu.CompilerParams(vmem_limit_bytes=16 * 2**20),
        name="write",
    )(new_error, whole, total)


def solution(mesh):
    in_specs = (P("dp", None, None), P("dp", None, "mp"), P("dp", None, "mp"), P(None, "mp"))
    out_specs = (P("dp", None, "mp"), P(None, "mp"))
    return jax.shard_map(
        per_device, mesh=mesh, in_specs=in_specs, out_specs=out_specs, check_vma=False
    )
```
